512 devices in a mesh: op: 16 (over z), sec: 32 (over y, x, core).
Axes of the slice: x: 4, y: 4, z: 16, core: 2. Of those that a mesh axis runs over, the one named last changes fastest.
Arguments:
- psi: bfloat16 [2, 64, 512, 512], P(None, 'sec'), may hold values from -6 to 6
- left_op: bfloat16 [48, 512, 512], P('op'), may hold values from -0.02734375 to 0.02734375
- right_op: bfloat16 [48, 512, 512], P('op'), may hold values from -0.25 to 0.25
- link: int32 [48, 64, 5], P('op', 'sec'), may hold values 0 or 1
Outputs:
- sigma: float32 [2, 64, 512, 512], P(None, 'sec', 'op')
The draws below stay inside these ranges and needn't reach their ends.
All inputs are finite; a program needn't handle non-finite values. No bound on the sum of `link` on one device may be relied on, other than what follows from the above.
Results may differ from the reference program's by a relative error of at most 0.0041.
Values may be sent and summed in bfloat16 or wider, within the bound.
No kernel may reach another device: no remote copies, remote signals or barrier semaphores. Data moves between devices by JAX's collectives and lax.ppermute only.
A program may use at most 64 MiB of HBM per device.

```python
import jax
import jax.numpy as jnp
from jax import lax

B = 512
REACH = 2
NSEC = 64
K = 48


def set_ends(array, stream_key, least, high):
    extent = array.shape
    spot = [jax.random.randint(jax.random.fold_in(stream_key, axis), (), 0, extent[axis]) for axis in range(len(extent))]
    array = array.at[tuple(spot)].set(least)
    longest = extent.index(max(extent))
    spot[longest] = (spot[longest] + 1) % extent[longest]
    return array.at[tuple(spot)].set(high)


def block_scale(stream_key, extent, split, least, largest):
    def one(dim, shards_of):
        steps = jax.random.uniform(jax.random.fold_in(jax.random.fold_in(stream_key, 6), dim), (shards_of,), jnp.float32, least / len(split), largest / len(split))
        return jnp.repeat(jnp.exp(steps), extent[dim] // shards_of).reshape((-1,) + (1,) * (len(extent) - dim - 1))

    level = one(*split[0])
    for cut in split[1:]:
        level = level * one(*cut)
    return level


def centred(rng, extent, scale, most, cuts=(), kind=jnp.bfloat16):
    level = block_scale(rng, extent, cuts, -0.22, 0.18) if cuts else 1.0
    values = jax.random.normal(rng, extent, jnp.float32) * scale * level
    return jnp.minimum(jnp.maximum(values, -most), most).astype(kind)


def setup_inputs(seed: int = 0) -> dict:
    key_of = jax.random.split(jax.random.key(seed), 5)
    return {
        "psi": centred(key_of[0], (2, NSEC, B, B), 1.0, 6.0, ((1, 32),)),
        "left_op": centred(key_of[1], (K, B, B), (B * K * 2) ** -0.5, 0.02734375, ((0, 16),)),
        "right_op": centred(key_of[2], (K, B, B), B ** -0.5, 0.25, ((0, 16),)),
        "link": set_ends((jax.random.randint(key_of[3], (K, NSEC, 2 * REACH + 1), 0, 2) < 1).astype(jnp.int32), jax.random.fold_in(key_of[3], 1), 0, 1),
    }


def reference(psi, left_op, right_op, link):
    padded = jnp.pad(psi, ((0, 0), (REACH, REACH), (0, 0), (0, 0)))

    def one_term(summed, position):
        links = link[position].astype(jnp.float32)
        combined = jnp.zeros((2, NSEC, B, B), jnp.float32)
        for offset in range(2 * REACH + 1):
            combined = combined + links[:, offset][None, :, None, None] * padded[:, offset:offset + NSEC].astype(jnp.float32)
        combined = combined.astype(jnp.bfloat16)
        halved = jnp.einsum("vtab,cb->vtac", combined.astype(jnp.float32), right_op[position].astype(jnp.float32)).astype(jnp.bfloat16)
        result = jnp.einsum("ea,vtac->vtec", left_op[position].astype(jnp.float32), halved.astype(jnp.float32))
        return summed + result, None

    start = jnp.zeros((2, NSEC, B, B), jnp.float32)
    summed, unused = lax.scan(one_term, start, jnp.arange(K))
    return summed
```

```python
import jax
import jax.numpy as jnp
from jax import lax
from jax.experimental import pallas as pl
from jax.experimental.pallas import tpu as pltpu
from jax.sharding import PartitionSpec as P

F32, BF16 = jnp.float32, jnp.bfloat16


def kernel(weight, across, own, chip, right, left, *rest):
    outs, (combined, halved) = rest[:4], rest[4:]
    terms, size = right.shape[0], right.shape[1]
    sources = (across, own, chip)
    v = pl.program_id(0)
    tile = 32
    for j in range(2):
        for start in range(0, size, tile):
            rows = pl.ds(start, tile)
            totals = [None] * terms
            for slot in range(6):
                block = sources[slot // 2][0, slot % 2, rows, :].astype(F32)
                for k in range(terms):
                    part = weight[k * 12 + j * 6 + slot] * block
                    totals[k] = part if totals[k] is None else totals[k] + part
            for k in range(terms):
                combined[k, rows, :] = totals[k].astype(BF16)
        for k in range(terms):
            halved[pl.ds(k * size, size), :] = jnp.dot(
                combined[k], right[k], preferred_element_type=F32
            ).astype(BF16)
        part = size // 4
        for c in range(4):
            outs[c][0, j] = jnp.dot(
                left[pl.ds(c * part, part), :], halved[...], preferred_element_type=F32
            ).astype(BF16)


def partials(weight, across, own, chip, right, left):
    terms, size = right.shape[0], right.shape[1]
    vectors = own.shape[0]
    source = pl.BlockSpec((1, 2, size, size), lambda v: (v, 0, 0, 0))
    share = pl.BlockSpec((1, 2, size // 4, size), lambda v: (v, 0, 0, 0))
    return pl.pallas_call(
        kernel,
        grid=(vectors,),
        in_specs=[
            pl.BlockSpec(memory_space=pltpu.SMEM),
            source,
            source,
            source,
            pl.BlockSpec(right.shape, lambda v: (0, 0, 0)),
            pl.BlockSpec(left.shape, lambda v: (0, 0)),
        ],
        out_specs=[share] * 4,
        out_shape=[jax.ShapeDtypeStruct((vectors, 2, size // 4, size), BF16)] * 4,
        scratch_shapes=[
            pltpu.VMEM((terms, size, size), BF16),
            pltpu.VMEM((terms * size, size), BF16),
        ],
        compiler_params=pltpu.CompilerParams(vmem_limit_bytes=40 * 2**20),
        cost_estimate=pl.CostEstimate(
            flops=4 * terms * vectors * 2 * size**3, bytes_accessed=12 * 2**20, transcendentals=0
        ),
    )(weight, across, own, chip, right, left)


def shards(psi, left_op, right_op, link):
    terms, size = left_op.shape[0], left_op.shape[1]
    z = lax.axis_index("op")
    place = lax.axis_index("sec")
    count = lax.axis_size("sec")
    core = place % 2

    chip = lax.ppermute(psi, "sec", [(i, i ^ 1) for i in range(count)])
    facing = [(i, (i + 1) % count) for i in range(1, count, 2)]
    across = lax.ppermute(psi, "sec", facing + [(b, a) for a, b in facing])

    window = jnp.stack([jnp.pad(link[:, j], ((0, 0), (j, 1 - j))) for j in range(2)], axis=1)
    slot = jnp.arange(6)
    outside = ((place == 0) & (slot < 2)) | ((place == count - 1) & (slot >= 4))
    window = jnp.where(outside, 0, window).astype(F32)
    swapped = jnp.concatenate([window[..., 4:], window[..., 2:4], window[..., :2]], axis=-1)
    weight = jnp.where(core == 0, window, swapped).reshape(-1)

    right = jnp.swapaxes(right_op, 1, 2)
    by_class = left_op.reshape(terms, 4, 4, size // 16, size)
    by_class = jnp.roll(by_class, -(z % 4), axis=2)
    left = by_class.transpose(2, 1, 3, 0, 4).reshape(size, terms * size)

    mine, up, two, down = partials(weight, across, psi, chip, right, left)

    def shift(x, by):
        n = lax.axis_size("op")
        return lax.ppermute(x, "op", [(i, (i + by) % n) for i in range(n)])

    up = shift(up, 1)
    down = shift(down, -1)
    two = jnp.stack([shift(two[:, 0], -2), shift(two[:, 1], 2)], axis=1)
    group = sum(x.astype(F32) for x in (mine, up, down, two)).astype(BF16)
    shares = group.reshape(2, 2, 4, size // 16, size).transpose(2, 0, 1, 3, 4)
    groups = [[a + 4 * i for i in range(4)] for a in range(4)]
    shares = lax.all_to_all(shares, "op", 0, 0, axis_index_groups=groups, tiled=True)
    return shares.astype(F32).sum(axis=0)


def solution(mesh):
    placed = (
        P(None, "sec", None, None),
        P("op", None, None),
        P("op", None, None),
        P("op", "sec", None),
    )
    return jax.shard_map(
        shards, mesh=mesh, in_specs=placed, out_specs=P(None, "sec", "op", None), check_vma=False
    )
```

```python
import jax
import jax.numpy as jnp
from jax import lax
from jax.experimental import pallas as pl
from jax.experimental.pallas import tpu as pltpu
from jax.sharding import PartitionSpec as P

F32, BF16 = jnp.float32, jnp.bfloat16
RING = 16
LEADERS = (0, 3, -3, 6, -6)
ORDER = [1 - p for p in LEADERS] + [-1 - p for p in LEADERS] + [-p for p in LEADERS] + [8]


def split_kernel(psi, *rest):
    outs, sems = rest[:-1], rest[-1]
    copies = [pltpu.make_async_copy(psi.at[v], out, sems.at[v]) for v, out in enumerate(outs)]
    for copy in copies:
        copy.start()
    for copy in copies:
        copy.wait()


def split(psi):
    vectors = psi.shape[0]
    return pl.pallas_call(
        split_kernel,
        in_specs=[pl.BlockSpec(memory_space=pl.ANY)],
        out_specs=[pl.BlockSpec(memory_space=pl.ANY)] * vectors,
        out_shape=[jax.ShapeDtypeStruct(psi.shape[1:], BF16)] * vectors,
        scratch_shapes=[pltpu.SemaphoreType.DMA((vectors,))],
        compiler_params=pltpu.CompilerParams(vmem_limit_bytes=56 * 2**20),
        cost_estimate=pl.CostEstimate(flops=0, bytes_accessed=4 * 2**20, transcendentals=0),
    )(psi)


def arrange_kernel(at, left, right, left_out, right_out):
    terms, size = left.shape[0], left.shape[1]
    share = size // RING
    sign = 1 - 2 * (at[0] % 2)
    for place, j in enumerate(ORDER):
        start = pl.multiple_of(lax.rem(at[2] + sign * j + RING, RING) * share, share)
        for k in range(terms):
            left_out[pl.ds(place * share, share), pl.ds(k * size, size)] = left[
                k, pl.ds(start, share), :
            ]
    for k in range(terms):
        right_out[k] = right[k].T


def arrange(at, left, right):
    terms, size = left.shape[0], left.shape[1]
    whole = pl.BlockSpec(memory_space=pltpu.VMEM)
    return pl.pallas_call(
        arrange_kernel,
        in_specs=[pl.BlockSpec(memory_space=pltpu.SMEM), whole, whole],
        out_specs=[whole, whole],
        out_shape=[
            jax.ShapeDtypeStruct((size, terms * size), BF16),
            jax.ShapeDtypeStruct(right.shape, BF16),
        ],
        compiler_params=pltpu.CompilerParams(vmem_limit_bytes=16 * 2**20),
        cost_estimate=pl.CostEstimate(flops=0, bytes_accessed=6 * 2**20, transcendentals=0),
    )(at, left, right)


def kernel(v, place, link, across, own, chip, right, left, up, down, mine, opposite, combined, halved):
    terms, size = right.shape[0], right.shape[1]
    first_core = place[0] % 2 == 0
    lowest, highest = place[0] == 0, place[0] == place[1] - 1
    half, tall, wide, high = size // 2, 16, 256, 128

    def weight(k, j, if_first, if_second):
        reach = jnp.where(first_core, if_first, if_second)
        outside = (lowest & (reach < 2 - j)) | (highest & (reach > 3 - j))
        return jnp.where(outside, 0, link[(k * 2 + j) * 5 + reach]).astype(F32)

    reaches = (((0, 4), (2, 2), (3, 3), (4, 0), (1, 1)), ((0, 4), (1, 1), (2, 2), (4, 0), (3, 3)))
    weights = [
        [[weight(k, j, *pair) for pair in reaches[j]] for k in range(terms)] for j in range(2)
    ]

    def combine(part):
        for row in range(0, half, tall):
            rows = pl.ds(part * half + row, tall)
            for column in range(0, size, wide):
                columns = pl.ds(column, wide)
                a0, a1 = (across[i, rows, columns].astype(F32) for i in range(2))
                o0, o1 = (own[i, rows, columns].astype(F32) for i in range(2))
                c0, c1 = (chip[v, i, rows, columns].astype(F32) for i in range(2))
                fifth = (jnp.where(first_core, a1, c1), jnp.where(first_core, c0, a0))
                for j, blocks in enumerate(((a0, o0, o1, c0, fifth[0]), (a1, o0, o1, c1, fifth[1]))):
                    for k in range(terms):
                        total = weights[j][k][0] * blocks[0]
                        for slot in range(1, 5):
                            total += weights[j][k][slot] * blocks[slot]
                        combined[part, j * terms + k, pl.ds(row, tall), columns] = total.astype(BF16)

    def multiply_right(part):
        for j in range(2):
            for k in range(terms):
                halved[j, pl.ds(k * size + part * half, half), :] = jnp.dot(
                    combined[part, j * terms + k], right[k], preferred_element_type=F32
                ).astype(BF16)

    combine(0)
    combine(1)
    multiply_right(0)
    multiply_right(1)
    for j in range(2):
        for top in range(0, size, high):
            sums = jnp.dot(
                left[pl.ds(top, high), :], halved[j], preferred_element_type=F32
            ).astype(BF16)
            start = 0
            for out in (up, down, mine, opposite):
                end = start + out.shape[1]
                low, stop = max(top, start), min(top + high, end)
                if low < stop:
                    out[j, pl.ds(low - start, stop - low)] = sums[low - top : stop - top]
                start = end


def partials(v, place, link, across, own, chip, right, left):
    terms, size = right.shape[0], right.shape[1]
    share = size // RING
    whole = pl.BlockSpec(memory_space=pltpu.VMEM)
    scalars = pl.BlockSpec(memory_space=pltpu.SMEM)
    counts = [len(LEADERS)] * 3 + [1]
    return pl.pallas_call(
        lambda *refs: kernel(v, *refs),
        in_specs=[scalars, scalars] + [whole] * 5,
        out_specs=[whole] * 4,
        out_shape=[jax.ShapeDtypeStruct((2, n * share, size), BF16) for n in counts],
        scratch_shapes=[
            pltpu.VMEM((2, 2 * terms, size // 2, size), BF16),
            pltpu.VMEM((2, terms * size, size), BF16),
        ],
        compiler_params=pltpu.CompilerParams(vmem_limit_bytes=32 * 2**20),
        cost_estimate=pl.CostEstimate(
            flops=8 * terms * size**3, bytes_accessed=8 * 2**20, transcendentals=0
        ),
    )(place, link, across, own, chip, right, left)


def shift(x, by):
    n, m = lax.axis_size("op"), lax.axis_size("sec")
    pairs = [
        (i * m + q, (i + (-by if q % 2 else by)) % n * m + q) for i in range(n) for q in range(m)
    ]
    return lax.ppermute(x, ("op", "sec"), pairs)


def shards(psi, left_op, right_op, link):
    place = lax.axis_index("sec")
    count = lax.axis_size("sec")
    vectors = psi.shape[0]
    share = psi.shape[2] // RING
    at = jnp.stack([place, count, lax.axis_index("op")]).astype(jnp.int32)

    facing = [(i, i + 1) for i in range(1, count - 1, 2)]
    facing += [(b, a) for a, b in facing]
    own = split(psi)
    across = [lax.ppermute(block, "sec", facing) for block in own]
    chip = lax.ppermute(psi, "sec", [(i, i ^ 1) for i in range(count)])

    left, right = arrange(at, left_op, right_op)
    totals, opposites = [], []
    for v in range(vectors):
        up, down, mine, opposite = partials(
            v, at, link.reshape(-1), across[v], own[v], chip, right, left
        )
        total = mine.astype(F32) + shift(up, 1).astype(F32) + shift(down, -1).astype(F32)
        totals.append(total.reshape(2, len(LEADERS), share, -1))
        opposites.append(opposite)
    opposite = shift(jnp.stack(opposites), -2).astype(F32)
    here, above, below, far_above, far_below = (
        jnp.stack([total[:, i] for total in totals]) for i in range(len(LEADERS))
    )
    far_above = shift((far_above + opposite).astype(BF16), -3).astype(F32)
    far_below = shift(far_below.astype(BF16), 3).astype(F32)
    above = shift((above + far_above).astype(BF16), -3).astype(F32)
    below = shift((below + far_below).astype(BF16), 3).astype(F32)
    return here + above + below


def solution(mesh):
    placed = (
        P(None, "sec", None, None),
        P("op", None, None),
        P("op", None, None),
        P("op", "sec", None),
    )
    return jax.shard_map(
        shards, mesh=mesh, in_specs=placed, out_specs=P(None, "sec", "op", None), check_vma=False
    )
```

```python
import jax
import jax.numpy as jnp
from jax import lax
from jax.experimental import pallas as pl
from jax.experimental.pallas import tpu as pltpu
from jax.sharding import PartitionSpec as P

F32, BF16 = jnp.float32, jnp.bfloat16
RING = 16
LEADERS = (0, 3, -3, 6, -6)
ORDER = [1 - p for p in LEADERS] + [-1 - p for p in LEADERS] + [-p for p in LEADERS] + [8]


def split_kernel(psi, *rest):
    outs, sems = rest[:-1], rest[-1]
    copies = [pltpu.make_async_copy(psi.at[v], out, sems.at[v]) for v, out in enumerate(outs)]
    for copy in copies:
        copy.start()
    for copy in copies:
        copy.wait()


def split(psi):
    vectors = psi.shape[0]
    return pl.pallas_call(
        split_kernel,
        in_specs=[pl.BlockSpec(memory_space=pl.ANY)],
        out_specs=[pl.BlockSpec(memory_space=pltpu.VMEM)] * vectors,
        out_shape=[jax.ShapeDtypeStruct(psi.shape[1:], BF16)] * vectors,
        scratch_shapes=[pltpu.SemaphoreType.DMA((vectors,))],
        compiler_params=pltpu.CompilerParams(vmem_limit_bytes=60 * 10**6),
        cost_estimate=pl.CostEstimate(flops=0, bytes_accessed=4 * 2**20, transcendentals=0),
    )(psi)


def arrange_kernel(at, left, right, left_out, right_out):
    terms, size = left.shape[0], left.shape[1]
    share = size // RING
    sign = 1 - 2 * (at[0] % 2)
    for place, j in enumerate(ORDER):
        start = pl.multiple_of(lax.rem(at[2] + sign * j + RING, RING) * share, share)
        for k in range(terms):
            left_out[pl.ds(place * share, share), pl.ds(k * size, size)] = left[
                k, pl.ds(start, share), :
            ]
    for k in range(terms):
        right_out[k] = right[k].T


def arrange(at, left, right):
    terms, size = left.shape[0], left.shape[1]
    whole = pl.BlockSpec(memory_space=pltpu.VMEM)
    return pl.pallas_call(
        arrange_kernel,
        in_specs=[pl.BlockSpec(memory_space=pltpu.SMEM), whole, whole],
        out_specs=[whole, whole],
        out_shape=[
            jax.ShapeDtypeStruct((size, terms * size), BF16),
            jax.ShapeDtypeStruct(right.shape, BF16),
        ],
        compiler_params=pltpu.CompilerParams(vmem_limit_bytes=16 * 2**20),
        cost_estimate=pl.CostEstimate(flops=0, bytes_accessed=6 * 2**20, transcendentals=0),
    )(at, left, right)


def kernel(v, place, link, across, own, chip, right, left, up, down, mine, opposite, combined, halved):
    terms, size = right.shape[0], right.shape[1]
    first_core = place[0] % 2 == 0
    lowest, highest = place[0] == 0, place[0] == place[1] - 1
    half, tall, wide, high = size // 2, 16, 256, 128

    def weight(k, j, if_first, if_second):
        reach = jnp.where(first_core, if_first, if_second)
        outside = (lowest & (reach < 2 - j)) | (highest & (reach > 3 - j))
        return jnp.where(outside, 0, link[(k * 2 + j) * 5 + reach]).astype(F32)

    reaches = (((0, 4), (2, 2), (3, 3), (4, 0), (1, 1)), ((0, 4), (1, 1), (2, 2), (4, 0), (3, 3)))
    weights = [
        [[weight(k, j, *pair) for pair in reaches[j]] for k in range(terms)] for j in range(2)
    ]

    def combine(part):
        for row in range(0, half, tall):
            rows = pl.ds(part * half + row, tall)
            for column in range(0, size, wide):
                columns = pl.ds(column, wide)
                a0, a1 = (across[i, rows, columns].astype(F32) for i in range(2))
                o0, o1 = (own[i, rows, columns].astype(F32) for i in range(2))
                c0, c1 = (chip[v, i, rows, columns].astype(F32) for i in range(2))
                fifth = (jnp.where(first_core, a1, c1), jnp.where(first_core, c0, a0))
                for j, blocks in enumerate(((a0, o0, o1, c0, fifth[0]), (a1, o0, o1, c1, fifth[1]))):
                    for k in range(terms):
                        total = weights[j][k][0] * blocks[0]
                        for slot in range(1, 5):
                            total += weights[j][k][slot] * blocks[slot]
                        combined[part, j * terms + k, pl.ds(row, tall), columns] = total.astype(BF16)

    def multiply_right(part):
        for j in range(2):
            for k in range(terms):
                halved[j, pl.ds(k * size + part * half, half), :] = jnp.dot(
                    combined[part, j * terms + k], right[k], preferred_element_type=F32
                ).astype(BF16)

    combine(0)
    combine(1)
    multiply_right(0)
    multiply_right(1)
    for j in range(2):
        for top in range(0, size, high):
            sums = jnp.dot(
                left[pl.ds(top, high), :], halved[j], preferred_element_type=F32
            ).astype(BF16)
            start = 0
            for out in (up, down, mine, opposite):
                end = start + out.shape[1]
                low, stop = max(top, start), min(top + high, end)
                if low < stop:
                    out[j, pl.ds(low - start, stop - low)] = sums[low - top : stop - top]
                start = end


def partials(v, place, link, across, own, chip, right, left):
    terms, size = right.shape[0], right.shape[1]
    share = size // RING
    whole = pl.BlockSpec(memory_space=pltpu.VMEM)
    scalars = pl.BlockSpec(memory_space=pltpu.SMEM)
    counts = [len(LEADERS)] * 3 + [1]
    return pl.pallas_call(
        lambda *refs: kernel(v, *refs),
        in_specs=[scalars, scalars] + [whole] * 5,
        out_specs=[whole] * 4,
        out_shape=[jax.ShapeDtypeStruct((2, n * share, size), BF16) for n in counts],
        scratch_shapes=[
            pltpu.VMEM((2, 2 * terms, size // 2, size), BF16),
            pltpu.VMEM((2, terms * size, size), BF16),
        ],
        compiler_params=pltpu.CompilerParams(vmem_limit_bytes=32 * 2**20),
        cost_estimate=pl.CostEstimate(
            flops=8 * terms * size**3, bytes_accessed=8 * 2**20, transcendentals=0
        ),
    )(place, link, across, own, chip, right, left)


def shift(x, by):
    n, m = lax.axis_size("op"), lax.axis_size("sec")
    pairs = [
        (i * m + q, (i + (-by if q % 2 else by)) % n * m + q) for i in range(n) for q in range(m)
    ]
    return lax.ppermute(x, ("op", "sec"), pairs)


def shards(psi, left_op, right_op, link):
    place = lax.axis_index("sec")
    count = lax.axis_size("sec")
    vectors = psi.shape[0]
    share = psi.shape[2] // RING
    at = jnp.stack([place, count, lax.axis_index("op")]).astype(jnp.int32)

    facing = [(i, i + 1) for i in range(1, count - 1, 2)]
    facing += [(b, a) for a, b in facing]
    own = split(psi)
    across = [lax.ppermute(block, "sec", facing) for block in own]
    chip = lax.ppermute(psi, "sec", [(i, i ^ 1) for i in range(count)])

    left, right = arrange(at, left_op, right_op)
    totals, opposites = [], []
    for v in range(vectors):
        up, down, mine, opposite = partials(
            v, at, link.reshape(-1), across[v], own[v], chip, right, left
        )
        total = mine.astype(F32) + shift(up, 1).astype(F32) + shift(down, -1).astype(F32)
        totals.append(total.reshape(2, len(LEADERS), share, -1))
        opposites.append(opposite)
    opposite = shift(jnp.stack(opposites), -2).astype(F32)
    here, above, below, far_above, far_below = (
        jnp.stack([total[:, i] for total in totals]) for i in range(len(LEADERS))
    )
    far_above = shift((far_above + opposite).astype(BF16), -3).astype(F32)
    far_below = shift(far_below.astype(BF16), 3).astype(F32)
    above = shift((above + far_above).astype(BF16), -3).astype(F32)
    below = shift((below + far_below).astype(BF16), 3).astype(F32)
    return here + above + below


def solution(mesh):
    placed = (
        P(None, "sec", None, None),
        P("op", None, None),
        P("op", None, None),
        P("op", "sec", None),
    )
    return jax.shard_map(
        shards, mesh=mesh, in_specs=placed, out_specs=P(None, "sec", "op", None), check_vma=False
    )
```

```python
import functools

import jax
import jax.numpy as jnp
from jax import lax
from jax.experimental import pallas as pl
from jax.experimental.pallas import tpu as pltpu
from jax.sharding import PartitionSpec as P

F32, BF16 = jnp.float32, jnp.bfloat16
RING = 16
LEADERS = (0, 4, -3, 7, -6)
SPARE = 2
ORDER = [1 - p for p in LEADERS] + [-1 - p for p in LEADERS] + [-p for p in LEADERS] + [-SPARE]


def split_kernel(psi, *rest):
    outs, sems = rest[:-1], rest[-1]
    copies = [pltpu.make_async_copy(psi.at[v], out, sems.at[v]) for v, out in enumerate(outs)]
    for copy in copies:
        copy.start()
    for copy in copies:
        copy.wait()


def split(psi):
    vectors = psi.shape[0]
    return pl.pallas_call(
        split_kernel,
        in_specs=[pl.BlockSpec(memory_space=pl.ANY)],
        out_specs=[pl.BlockSpec(memory_space=pltpu.VMEM)] * vectors,
        out_shape=[jax.ShapeDtypeStruct(psi.shape[1:], BF16)] * vectors,
        scratch_shapes=[pltpu.SemaphoreType.DMA((vectors,))],
        compiler_params=pltpu.CompilerParams(vmem_limit_bytes=60 * 10**6),
        cost_estimate=pl.CostEstimate(flops=0, bytes_accessed=4 * 2**20, transcendentals=0),
    )(psi)


def arrange_kernel(at, left, right, left_out, right_out):
    terms, size = left.shape[0], left.shape[1]
    share = size // RING
    sign = 1 - 2 * (at[0] % 2)
    for place, j in enumerate(ORDER):
        start = pl.multiple_of(lax.rem(at[2] + sign * j + RING, RING) * share, share)
        for k in range(terms):
            left_out[pl.ds(place * share, share), pl.ds(k * size, size)] = left[
                k, pl.ds(start, share), :
            ]
    for k in range(terms):
        right_out[k] = right[k].T


def arrange(at, left, right):
    terms, size = left.shape[0], left.shape[1]
    whole = pl.BlockSpec(memory_space=pltpu.VMEM)
    return pl.pallas_call(
        arrange_kernel,
        in_specs=[pl.BlockSpec(memory_space=pltpu.SMEM), whole, whole],
        out_specs=[whole, whole],
        out_shape=[
            jax.ShapeDtypeStruct((size, terms * size), BF16),
            jax.ShapeDtypeStruct(right.shape, BF16),
        ],
        compiler_params=pltpu.CompilerParams(vmem_limit_bytes=16 * 2**20),
        cost_estimate=pl.CostEstimate(flops=0, bytes_accessed=6 * 2**20, transcendentals=0),
    )(at, left, right)


def kernel(v, place, link, across, own, chip, right, left, *rest):
    earlier, outs, (combined, halved) = rest[: 2 * v], rest[2 * v : -2], rest[-2:]
    up, down, mine, spare = outs
    if v:
        down[0], spare[0] = earlier[0][...], earlier[1][...]
        down, spare = down.at[1], spare.at[1]
    terms, size = right.shape[0], right.shape[1]
    first_core = place[0] % 2 == 0
    lowest, highest = place[0] == 0, place[0] == place[1] - 1
    half, tall, wide, high = size // 2, 16, 256, 128

    def weight(k, j, if_first, if_second):
        reach = jnp.where(first_core, if_first, if_second)
        outside = (lowest & (reach < 2 - j)) | (highest & (reach > 3 - j))
        return jnp.where(outside, 0, link[(k * 2 + j) * 5 + reach]).astype(F32)

    reaches = (((0, 4), (2, 2), (3, 3), (4, 0), (1, 1)), ((0, 4), (1, 1), (2, 2), (4, 0), (3, 3)))
    weights = [
        [[weight(k, j, *pair) for pair in reaches[j]] for k in range(terms)] for j in range(2)
    ]

    def combine(part):
        for row in range(0, half, tall):
            rows = pl.ds(part * half + row, tall)
            for column in range(0, size, wide):
                columns = pl.ds(column, wide)
                a0, a1 = (across[i, rows, columns].astype(F32) for i in range(2))
                o0, o1 = (own[i, rows, columns].astype(F32) for i in range(2))
                c0, c1 = (chip[v, i, rows, columns].astype(F32) for i in range(2))
                fifth = (jnp.where(first_core, a1, c1), jnp.where(first_core, c0, a0))
                for j, blocks in enumerate(((a0, o0, o1, c0, fifth[0]), (a1, o0, o1, c1, fifth[1]))):
                    for k in range(terms):
                        total = weights[j][k][0] * blocks[0]
                        for slot in range(1, 5):
                            total += weights[j][k][slot] * blocks[slot]
                        combined[part, j * terms + k, pl.ds(row, tall), columns] = total.astype(BF16)

    def multiply_right(part):
        for j in range(2):
            for k in range(terms):
                halved[j, pl.ds(k * size + part * half, half), :] = jnp.dot(
                    combined[part, j * terms + k], right[k], preferred_element_type=F32
                ).astype(BF16)

    combine(0)
    combine(1)
    multiply_right(0)
    multiply_right(1)
    for j in range(2):
        for top in range(0, size, high):
            sums = jnp.dot(
                left[pl.ds(top, high), :], halved[j], preferred_element_type=F32
            ).astype(BF16)
            start = 0
            for out in (up, down, mine, spare):
                end = start + out.shape[1]
                low, stop = max(top, start), min(top + high, end)
                if low < stop:
                    out[j, pl.ds(low - start, stop - low)] = sums[low - top : stop - top]
                start = end


def partials(v, place, link, across, own, chip, right, left, earlier=()):
    terms, size = right.shape[0], right.shape[1]
    share = size // RING
    whole = pl.BlockSpec(memory_space=pltpu.VMEM)
    scalars = pl.BlockSpec(memory_space=pltpu.SMEM)
    many, one = (2, len(LEADERS) * share, size), (2, share, size)
    both = (2,) * v
    shapes = [many, both + many, many, both + one]
    return pl.pallas_call(
        functools.partial(kernel, v),
        in_specs=[scalars, scalars] + [whole] * (5 + len(earlier)),
        out_specs=[whole] * 4,
        out_shape=[jax.ShapeDtypeStruct(shape, BF16) for shape in shapes],
        scratch_shapes=[
            pltpu.VMEM((2, 2 * terms, size // 2, size), BF16),
            pltpu.VMEM((2, terms * size, size), BF16),
        ],
        compiler_params=pltpu.CompilerParams(vmem_limit_bytes=32 * 2**20),
        cost_estimate=pl.CostEstimate(
            flops=8 * terms * size**3, bytes_accessed=8 * 2**20, transcendentals=0
        ),
    )(place, link, across, own, chip, right, left, *earlier)


def shift(x, by):
    n, m = lax.axis_size("op"), lax.axis_size("sec")
    pairs = [
        (i * m + q, (i + (-by if q % 2 else by)) % n * m + q) for i in range(n) for q in range(m)
    ]
    return lax.ppermute(x, ("op", "sec"), pairs)


def shards(psi, left_op, right_op, link):
    place = lax.axis_index("sec")
    count = lax.axis_size("sec")
    share = psi.shape[2] // RING
    at = jnp.stack([place, count, lax.axis_index("op")]).astype(jnp.int32)

    facing = [(i, i + 1) for i in range(1, count - 1, 2)]
    facing += [(b, a) for a, b in facing]
    own = split(psi)
    across = [lax.ppermute(block, "sec", facing) for block in own]
    chip = lax.ppermute(psi, "sec", [(i, i ^ 1) for i in range(count)])

    left, right = arrange(at, left_op, right_op)
    link = link.reshape(-1)
    up0, down, mine0, spare = partials(0, at, link, across[0], own[0], chip, right, left)
    up0 = shift(up0, 1)
    up1, down, mine1, spare = partials(
        1, at, link, across[1], own[1], chip, right, left, (down, spare)
    )
    up1 = shift(up1, 1)
    down = shift(down, -1)
    spare = shift(spare, -SPARE)
    total = jnp.stack(
        [x.astype(F32) + y.astype(F32) + z.astype(F32) for x, y, z in ((mine0, up0, down[0]), (mine1, up1, down[1]))]
    ).reshape(2, 2, len(LEADERS), share, -1)
    far_above = shift(total[:, :, 3].astype(BF16), -3).astype(F32)
    far_below = shift(total[:, :, 4].astype(BF16), 3).astype(F32)
    above = shift((total[:, :, 1] + far_above).astype(BF16), -4).astype(F32)
    below = shift((total[:, :, 2] + far_below).astype(BF16), 3).astype(F32)
    return total[:, :, 0] + spare.astype(F32) + above + below


def solution(mesh):
    placed = (
        P(None, "sec", None, None),
        P("op", None, None),
        P("op", None, None),
        P("op", "sec", None),
    )
    return jax.shard_map(
        shards, mesh=mesh, in_specs=placed, out_specs=P(None, "sec", "op", None), check_vma=False
    )
```

```python
import functools

import jax
import jax.numpy as jnp
from jax import lax
from jax.experimental import pallas as pl
from jax.experimental.pallas import tpu as pltpu
from jax.sharding import PartitionSpec as P

F32, BF16 = jnp.float32, jnp.bfloat16
RING = 16
LEADERS = (0, 4, -3, 7, -6)
SPARE = 2
ORDER = [1 - p for p in LEADERS] + [-1 - p for p in LEADERS] + [-p for p in LEADERS] + [-SPARE]


def split_kernel(psi, *rest):
    outs, sems = rest[:-1], rest[-1]
    copies = [pltpu.make_async_copy(psi.at[v], out, sems.at[v]) for v, out in enumerate(outs)]
    for copy in copies:
        copy.start()
    for copy in copies:
        copy.wait()


def split(psi):
    vectors = psi.shape[0]
    return pl.pallas_call(
        split_kernel,
        in_specs=[pl.BlockSpec(memory_space=pl.ANY)],
        out_specs=[pl.BlockSpec(memory_space=pltpu.VMEM)] * vectors,
        out_shape=[jax.ShapeDtypeStruct(psi.shape[1:], BF16)] * vectors,
        scratch_shapes=[pltpu.SemaphoreType.DMA((vectors,))],
        compiler_params=pltpu.CompilerParams(vmem_limit_bytes=60 * 10**6),
        cost_estimate=pl.CostEstimate(flops=0, bytes_accessed=4 * 2**20, transcendentals=0),
    )(psi)


def arrange_kernel(at, left, right, left_out, right_out):
    terms, size = left.shape[0], left.shape[1]
    share = size // RING
    sign = 1 - 2 * (at[0] % 2)
    for place, j in enumerate(ORDER):
        start = pl.multiple_of(lax.rem(at[2] + sign * j + RING, RING) * share, share)
        for k in range(terms):
            left_out[pl.ds(place * share, share), pl.ds(k * size, size)] = left[
                k, pl.ds(start, share), :
            ]
    for k in range(terms):
        right_out[k] = right[k].T


def arrange(at, left, right):
    terms, size = left.shape[0], left.shape[1]
    whole = pl.BlockSpec(memory_space=pltpu.VMEM)
    return pl.pallas_call(
        arrange_kernel,
        in_specs=[pl.BlockSpec(memory_space=pltpu.SMEM), whole, whole],
        out_specs=[whole, whole],
        out_shape=[
            jax.ShapeDtypeStruct((size, terms * size), BF16),
            jax.ShapeDtypeStruct(right.shape, BF16),
        ],
        compiler_params=pltpu.CompilerParams(vmem_limit_bytes=16 * 2**20),
        cost_estimate=pl.CostEstimate(flops=0, bytes_accessed=6 * 2**20, transcendentals=0),
    )(at, left, right)


def kernel(v, place, link, across, own, chip, right, left, up, down, mine, spare, combined, halved):
    terms, size = right.shape[0], right.shape[1]
    first_core = place[0] % 2 == 0
    lowest, highest = place[0] == 0, place[0] == place[1] - 1
    half, tall, wide, high = size // 2, 16, 256, 128

    def weight(k, j, if_first, if_second):
        reach = jnp.where(first_core, if_first, if_second)
        outside = (lowest & (reach < 2 - j)) | (highest & (reach > 3 - j))
        return jnp.where(outside, 0, link[(k * 2 + j) * 5 + reach]).astype(F32)

    reaches = (((0, 4), (2, 2), (3, 3), (4, 0), (1, 1)), ((0, 4), (1, 1), (2, 2), (4, 0), (3, 3)))
    weights = [
        [[weight(k, j, *pair) for pair in reaches[j]] for k in range(terms)] for j in range(2)
    ]

    def combine(part):
        for row in range(0, half, tall):
            rows = pl.ds(part * half + row, tall)
            for column in range(0, size, wide):
                columns = pl.ds(column, wide)
                a0, a1 = (across[i, rows, columns].astype(F32) for i in range(2))
                o0, o1 = (own[i, rows, columns].astype(F32) for i in range(2))
                c0, c1 = (chip[v, i, rows, columns].astype(F32) for i in range(2))
                fifth = (jnp.where(first_core, a1, c1), jnp.where(first_core, c0, a0))
                for j, blocks in enumerate(((a0, o0, o1, c0, fifth[0]), (a1, o0, o1, c1, fifth[1]))):
                    for k in range(terms):
                        total = weights[j][k][0] * blocks[0]
                        for slot in range(1, 5):
                            total += weights[j][k][slot] * blocks[slot]
                        combined[part, j * terms + k, pl.ds(row, tall), columns] = total.astype(BF16)

    def multiply_right(part):
        for j in range(2):
            for k in range(terms):
                halved[j, pl.ds(k * size + part * half, half), :] = jnp.dot(
                    combined[part, j * terms + k], right[k], preferred_element_type=F32
                ).astype(BF16)

    combine(0)
    combine(1)
    multiply_right(0)
    multiply_right(1)
    for j in range(2):
        for top in range(0, size, high):
            sums = jnp.dot(
                left[pl.ds(top, high), :], halved[j], preferred_element_type=F32
            ).astype(BF16)
            start = 0
            for out in (up, down, mine, spare):
                end = start + out.shape[1]
                low, stop = max(top, start), min(top + high, end)
                if low < stop:
                    out[j, pl.ds(low - start, stop - low)] = sums[low - top : stop - top]
                start = end


def partials(v, place, link, across, own, chip, right, left):
    terms, size = right.shape[0], right.shape[1]
    share = size // RING
    whole = pl.BlockSpec(memory_space=pltpu.VMEM)
    scalars = pl.BlockSpec(memory_space=pltpu.SMEM)
    counts = [len(LEADERS)] * 3 + [1]
    return pl.pallas_call(
        functools.partial(kernel, v),
        in_specs=[scalars, scalars] + [whole] * 5,
        out_specs=[whole] * 4,
        out_shape=[jax.ShapeDtypeStruct((2, n * share, size), BF16) for n in counts],
        scratch_shapes=[
            pltpu.VMEM((2, 2 * terms, size // 2, size), BF16),
            pltpu.VMEM((2, terms * size, size), BF16),
        ],
        compiler_params=pltpu.CompilerParams(vmem_limit_bytes=32 * 2**20),
        cost_estimate=pl.CostEstimate(
            flops=8 * terms * size**3, bytes_accessed=8 * 2**20, transcendentals=0
        ),
    )(place, link, across, own, chip, right, left)


def shift(x, by):
    n, m = lax.axis_size("op"), lax.axis_size("sec")
    pairs = [
        (i * m + q, (i + (-by if q % 2 else by)) % n * m + q) for i in range(n) for q in range(m)
    ]
    return lax.ppermute(x, ("op", "sec"), pairs)


def shards(psi, left_op, right_op, link):
    place = lax.axis_index("sec")
    count = lax.axis_size("sec")
    share = psi.shape[2] // RING
    at = jnp.stack([place, count, lax.axis_index("op")]).astype(jnp.int32)

    facing = [(i, i + 1) for i in range(1, count - 1, 2)]
    facing += [(b, a) for a, b in facing]
    own = split(psi)
    across = [lax.ppermute(block, "sec", facing) for block in own]
    chip = lax.ppermute(psi, "sec", [(i, i ^ 1) for i in range(count)])

    left, right = arrange(at, left_op, right_op)
    link = link.reshape(-1)
    here, above, below, spares = [], [], [], []
    for v in range(2):
        up, down, mine, spare = partials(v, at, link, across[v], own[v], chip, right, left)
        total = mine.astype(F32) + shift(up, 1).astype(F32) + shift(down, -1).astype(F32)
        total = total.reshape(2, len(LEADERS), share, -1)
        far_above = shift(total[:, 3].astype(BF16), -3).astype(F32)
        far_below = shift(total[:, 4].astype(BF16), 3).astype(F32)
        here.append(total[:, 0])
        above.append((total[:, 1] + far_above).astype(BF16))
        below.append((total[:, 2] + far_below).astype(BF16))
        spares.append(spare)
    spare = shift(jnp.stack(spares), -SPARE).astype(F32)
    above = shift(jnp.stack(above), -4).astype(F32)
    below = shift(jnp.stack(below), 3).astype(F32)
    return jnp.stack(here) + spare + above + below


def solution(mesh):
    placed = (
        P(None, "sec", None, None),
        P("op", None, None),
        P("op", None, None),
        P("op", "sec", None),
    )
    return jax.shard_map(
        shards, mesh=mesh, in_specs=placed, out_specs=P(None, "sec", "op", None), check_vma=False
    )
```

```python
import jax
import jax.numpy as jnp
from jax import lax
from jax.experimental import pallas as pl
from jax.experimental.pallas import tpu as pltpu
from jax.sharding import PartitionSpec as P

F32, BF16 = jnp.float32, jnp.bfloat16
RING = 16
LEADERS = (0, 4, -3, 7, -6)
SPARE = 2
ORDER = [1 - p for p in LEADERS] + [-1 - p for p in LEADERS] + [-p for p in LEADERS] + [-SPARE]


def take(psi, v, after=None):
    operands = [psi] + [x for x in (after,) if x is not None]

    def kernel(source, *rest):
        copy = pltpu.make_async_copy(source.at[v], rest[-2], rest[-1])
        copy.start()
        copy.wait()

    return pl.pallas_call(
        kernel,
        in_specs=[pl.BlockSpec(memory_space=pl.ANY)] * len(operands),
        out_specs=pl.BlockSpec(memory_space=pltpu.VMEM),
        out_shape=jax.ShapeDtypeStruct(psi.shape[1:], BF16),
        scratch_shapes=[pltpu.SemaphoreType.DMA],
        compiler_params=pltpu.CompilerParams(vmem_limit_bytes=60 * 10**6),
        cost_estimate=pl.CostEstimate(flops=0, bytes_accessed=4 * 2**20, transcendentals=0),
    )(*operands)


def arrange_kernel(at, left, right, left_out, right_out):
    terms, size = left.shape[0], left.shape[1]
    share = size // RING
    sign = 1 - 2 * (at[0] % 2)
    for place, j in enumerate(ORDER):
        start = pl.multiple_of(lax.rem(at[2] + sign * j + RING, RING) * share, share)
        for k in range(terms):
            left_out[pl.ds(place * share, share), pl.ds(k * size, size)] = left[
                k, pl.ds(start, share), :
            ]
    for k in range(terms):
        right_out[k] = right[k].T


def arrange(at, left, right):
    terms, size = left.shape[0], left.shape[1]
    whole = pl.BlockSpec(memory_space=pltpu.VMEM)
    return pl.pallas_call(
        arrange_kernel,
        in_specs=[pl.BlockSpec(memory_space=pltpu.SMEM), whole, whole],
        out_specs=[whole, whole],
        out_shape=[
            jax.ShapeDtypeStruct((size, terms * size), BF16),
            jax.ShapeDtypeStruct(right.shape, BF16),
        ],
        compiler_params=pltpu.CompilerParams(vmem_limit_bytes=16 * 2**20),
        cost_estimate=pl.CostEstimate(flops=0, bytes_accessed=6 * 2**20, transcendentals=0),
    )(at, left, right)


def kernel(place, link, chip, own, across, right, left, up, down, mine, spare, combined, halved):
    terms, size = right.shape[0], right.shape[1]
    first_core = place[0] % 2 == 0
    lowest, highest = place[0] == 0, place[0] == place[1] - 1
    half, tall, wide, high = size // 2, 16, 256, 128

    def weight(k, j, if_first, if_second):
        reach = jnp.where(first_core, if_first, if_second)
        outside = (lowest & (reach < 2 - j)) | (highest & (reach > 3 - j))
        return jnp.where(outside, 0, link[(k * 2 + j) * 5 + reach]).astype(F32)

    reaches = (((0, 4), (2, 2), (3, 3), (4, 0), (1, 1)), ((0, 4), (1, 1), (2, 2), (4, 0), (3, 3)))
    weights = [
        [[weight(k, j, *pair) for pair in reaches[j]] for k in range(terms)] for j in range(2)
    ]

    def combine(part):
        for row in range(0, half, tall):
            rows = pl.ds(part * half + row, tall)
            for column in range(0, size, wide):
                columns = pl.ds(column, wide)
                a0, a1 = (across[i, rows, columns].astype(F32) for i in range(2))
                o0, o1 = (own[i, rows, columns].astype(F32) for i in range(2))
                c0, c1 = (chip[i, rows, columns].astype(F32) for i in range(2))
                fifth = (jnp.where(first_core, a1, c1), jnp.where(first_core, c0, a0))
                for j, blocks in enumerate(((a0, o0, o1, c0, fifth[0]), (a1, o0, o1, c1, fifth[1]))):
                    for k in range(terms):
                        total = weights[j][k][0] * blocks[0]
                        for slot in range(1, 5):
                            total += weights[j][k][slot] * blocks[slot]
                        combined[part, j * terms + k, pl.ds(row, tall), columns] = total.astype(BF16)

    def multiply_right(part):
        for j in range(2):
            for k in range(terms):
                halved[j, pl.ds(k * size + part * half, half), :] = jnp.dot(
                    combined[part, j * terms + k], right[k], preferred_element_type=F32
                ).astype(BF16)

    combine(0)
    combine(1)
    multiply_right(0)
    multiply_right(1)
    for j in range(2):
        for top in range(0, size, high):
            sums = jnp.dot(
                left[pl.ds(top, high), :], halved[j], preferred_element_type=F32
            ).astype(BF16)
            start = 0
            for out in (up, down, mine, spare):
                end = start + out.shape[1]
                low, stop = max(top, start), min(top + high, end)
                if low < stop:
                    out[j, pl.ds(low - start, stop - low)] = sums[low - top : stop - top]
                start = end


def partials(place, link, across, own, chip, right, left):
    terms, size = right.shape[0], right.shape[1]
    share = size // RING
    whole = pl.BlockSpec(memory_space=pltpu.VMEM)
    scalars = pl.BlockSpec(memory_space=pltpu.SMEM)
    counts = [len(LEADERS)] * 3 + [1]
    return pl.pallas_call(
        kernel,
        in_specs=[scalars, scalars] + [whole] * 5,
        out_specs=[whole] * 4,
        out_shape=[jax.ShapeDtypeStruct((2, n * share, size), BF16) for n in counts],
        scratch_shapes=[
            pltpu.VMEM((2, 2 * terms, size // 2, size), BF16),
            pltpu.VMEM((2, terms * size, size), BF16),
        ],
        compiler_params=pltpu.CompilerParams(vmem_limit_bytes=32 * 2**20),
        cost_estimate=pl.CostEstimate(
            flops=8 * terms * size**3, bytes_accessed=8 * 2**20, transcendentals=0
        ),
    )(place, link, chip, own, across, right, left)


def shift(x, by):
    n, m = lax.axis_size("op"), lax.axis_size("sec")
    pairs = [
        (i * m + q, (i + (-by if q % 2 else by)) % n * m + q) for i in range(n) for q in range(m)
    ]
    return lax.ppermute(x, ("op", "sec"), pairs)


def shards(psi, left_op, right_op, link):
    place = lax.axis_index("sec")
    count = lax.axis_size("sec")
    share = psi.shape[2] // RING
    at = jnp.stack([place, count, lax.axis_index("op")]).astype(jnp.int32)

    facing = [(i, i + 1) for i in range(1, count - 1, 2)]
    facing += [(b, a) for a, b in facing]
    left, right = arrange(at, left_op, right_op)
    first = take(psi, 0)
    across = [lax.ppermute(first, "sec", facing)]
    second = take(psi, 1, left)
    across.append(lax.ppermute(second, "sec", facing))
    own = (first, second)
    chip = [lax.ppermute(x, "sec", [(i, i ^ 1) for i in range(count)]) for x in own]

    link = link.reshape(-1)
    totals, spares = [], []
    for v in range(2):
        up, down, mine, spare = partials(at, link, across[v], own[v], chip[v], right, left)
        total = mine.astype(F32) + shift(up, 1).astype(F32) + shift(down, -1).astype(F32)
        totals.append(total)
        spares.append(spare)
    total = jnp.stack(totals).reshape(2, 2, len(LEADERS), share, -1)
    spare = shift(jnp.stack(spares), -SPARE).astype(F32)
    far_above = shift(total[:, :, 3].astype(BF16), -3).astype(F32)
    far_below = shift(total[:, :, 4].astype(BF16), 3).astype(F32)
    above = shift((total[:, :, 1] + far_above).astype(BF16), -4).astype(F32)
    below = shift((total[:, :, 2] + far_below).astype(BF16), 3).astype(F32)
    return total[:, :, 0] + spare + above + below


def solution(mesh):
    placed = (
        P(None, "sec", None, None),
        P("op", None, None),
        P("op", None, None),
        P("op", "sec", None),
    )
    return jax.shard_map(
        shards, mesh=mesh, in_specs=placed, out_specs=P(None, "sec", "op", None), check_vma=False
    )
```

```python
import jax
import jax.numpy as jnp
from jax import lax
from jax.experimental import pallas as pl
from jax.experimental.pallas import tpu as pltpu
from jax.sharding import PartitionSpec as P

F32, BF16 = jnp.float32, jnp.bfloat16
RING = 16
LEADERS = (0, 3, -3, 6, -6)
ORDER = [1 - p for p in LEADERS] + [-1 - p for p in LEADERS] + [-p for p in LEADERS] + [8]


def split_kernel(psi, *rest):
    outs, sems = rest[:-1], rest[-1]
    copies = [pltpu.make_async_copy(psi.at[v], out, sems.at[v]) for v, out in enumerate(outs)]
    for copy in copies:
        copy.start()
    for copy in copies:
        copy.wait()


def split(psi):
    vectors = psi.shape[0]
    return pl.pallas_call(
        split_kernel,
        in_specs=[pl.BlockSpec(memory_space=pl.ANY)],
        out_specs=[pl.BlockSpec(memory_space=pltpu.VMEM)] * vectors,
        out_shape=[jax.ShapeDtypeStruct(psi.shape[1:], BF16)] * vectors,
        scratch_shapes=[pltpu.SemaphoreType.DMA((vectors,))],
        compiler_params=pltpu.CompilerParams(vmem_limit_bytes=60 * 10**6),
        cost_estimate=pl.CostEstimate(flops=0, bytes_accessed=4 * 2**20, transcendentals=0),
    )(psi)


def arrange_kernel(at, left, right, left_out, right_out):
    terms, size = left.shape[0], left.shape[1]
    share = size // RING
    sign = 1 - 2 * (at[0] % 2)
    for place, j in enumerate(ORDER):
        start = pl.multiple_of(lax.rem(at[2] + sign * j + RING, RING) * share, share)
        for k in range(terms):
            left_out[pl.ds(place * share, share), pl.ds(k * size, size)] = left[
                k, pl.ds(start, share), :
            ]
    for k in range(terms):
        right_out[k] = right[k].T


def arrange(at, left, right):
    terms, size = left.shape[0], left.shape[1]
    whole = pl.BlockSpec(memory_space=pltpu.VMEM)
    return pl.pallas_call(
        arrange_kernel,
        in_specs=[pl.BlockSpec(memory_space=pltpu.SMEM), whole, whole],
        out_specs=[whole, whole],
        out_shape=[
            jax.ShapeDtypeStruct((size, terms * size), BF16),
            jax.ShapeDtypeStruct(right.shape, BF16),
        ],
        compiler_params=pltpu.CompilerParams(vmem_limit_bytes=16 * 2**20),
        cost_estimate=pl.CostEstimate(flops=0, bytes_accessed=6 * 2**20, transcendentals=0),
    )(at, left, right)


def kernel(v, place, link, across, own, chip, right, left, up, down, mine, opposite, combined, halved):
    terms, size = right.shape[0], right.shape[1]
    first_core = place[0] % 2 == 0
    lowest, highest = place[0] == 0, place[0] == place[1] - 1
    half, tall, wide, high = size // 2, 16, 256, 128

    def weight(k, j, if_first, if_second):
        reach = jnp.where(first_core, if_first, if_second)
        outside = (lowest & (reach < 2 - j)) | (highest & (reach > 3 - j))
        return jnp.where(outside, 0, link[(k * 2 + j) * 5 + reach]).astype(F32)

    reaches = (((0, 4), (2, 2), (3, 3), (4, 0), (1, 1)), ((0, 4), (1, 1), (2, 2), (4, 0), (3, 3)))
    weights = [
        [[weight(k, j, *pair) for pair in reaches[j]] for k in range(terms)] for j in range(2)
    ]

    def combine(part):
        for row in range(0, half, tall):
            rows = pl.ds(part * half + row, tall)
            for column in range(0, size, wide):
                columns = pl.ds(column, wide)
                a0, a1 = (across[i, rows, columns].astype(F32) for i in range(2))
                o0, o1 = (own[i, rows, columns].astype(F32) for i in range(2))
                c0, c1 = (chip[i, rows, columns].astype(F32) for i in range(2))
                fifth = (jnp.where(first_core, a1, c1), jnp.where(first_core, c0, a0))
                for j, blocks in enumerate(((a0, o0, o1, c0, fifth[0]), (a1, o0, o1, c1, fifth[1]))):
                    for k in range(terms):
                        total = weights[j][k][0] * blocks[0]
                        for slot in range(1, 5):
                            total += weights[j][k][slot] * blocks[slot]
                        combined[part, j * terms + k, pl.ds(row, tall), columns] = total.astype(BF16)

    def multiply_right(part):
        for j in range(2):
            for k in range(terms):
                halved[j, pl.ds(k * size + part * half, half), :] = jnp.dot(
                    combined[part, j * terms + k], right[k], preferred_element_type=F32
                ).astype(BF16)

    combine(0)
    combine(1)
    multiply_right(0)
    multiply_right(1)
    for j in range(2):
        for top in range(0, size, high):
            sums = jnp.dot(
                left[pl.ds(top, high), :], halved[j], preferred_element_type=F32
            ).astype(BF16)
            start = 0
            for out in (up, down, mine, opposite):
                end = start + out.shape[1]
                low, stop = max(top, start), min(top + high, end)
                if low < stop:
                    out[j, pl.ds(low - start, stop - low)] = sums[low - top : stop - top]
                start = end


def partials(v, place, link, across, own, chip, right, left):
    terms, size = right.shape[0], right.shape[1]
    share = size // RING
    whole = pl.BlockSpec(memory_space=pltpu.VMEM)
    scalars = pl.BlockSpec(memory_space=pltpu.SMEM)
    counts = [len(LEADERS)] * 3 + [1]
    return pl.pallas_call(
        lambda *refs: kernel(v, *refs),
        in_specs=[scalars, scalars] + [whole] * 5,
        out_specs=[whole] * 4,
        out_shape=[jax.ShapeDtypeStruct((2, n * share, size), BF16) for n in counts],
        scratch_shapes=[
            pltpu.VMEM((2, 2 * terms, size // 2, size), BF16),
            pltpu.VMEM((2, terms * size, size), BF16),
        ],
        compiler_params=pltpu.CompilerParams(vmem_limit_bytes=32 * 2**20),
        cost_estimate=pl.CostEstimate(
            flops=8 * terms * size**3, bytes_accessed=8 * 2**20, transcendentals=0
        ),
    )(place, link, across, own, chip, right, left)


def shift(x, by):
    n, m = lax.axis_size("op"), lax.axis_size("sec")
    pairs = [
        (i * m + q, (i + (-by if q % 2 else by)) % n * m + q) for i in range(n) for q in range(m)
    ]
    return lax.ppermute(x, ("op", "sec"), pairs)


def shards(psi, left_op, right_op, link):
    place = lax.axis_index("sec")
    count = lax.axis_size("sec")
    vectors = psi.shape[0]
    share = psi.shape[2] // RING
    at = jnp.stack([place, count, lax.axis_index("op")]).astype(jnp.int32)

    facing = [(i, i + 1) for i in range(1, count - 1, 2)]
    facing += [(b, a) for a, b in facing]
    own = split(psi)
    across = [lax.ppermute(block, "sec", facing) for block in own]
    chip = [lax.ppermute(block, "sec", [(i, i ^ 1) for i in range(count)]) for block in own]

    left, right = arrange(at, left_op, right_op)
    totals, opposites = [], []
    for v in range(vectors):
        up, down, mine, opposite = partials(
            v, at, link.reshape(-1), across[v], own[v], chip[v], right, left
        )
        total = mine.astype(F32) + shift(up, 1).astype(F32) + shift(down, -1).astype(F32)
        totals.append(total.reshape(2, len(LEADERS), share, -1))
        opposites.append(opposite)
    opposite = shift(jnp.stack(opposites), -2).astype(F32)
    here, above, below, far_above, far_below = (
        jnp.stack([total[:, i] for total in totals]) for i in range(len(LEADERS))
    )
    far_above = shift((far_above + opposite).astype(BF16), -3).astype(F32)
    far_below = shift(far_below.astype(BF16), 3).astype(F32)
    above = shift((above + far_above).astype(BF16), -3).astype(F32)
    below = shift((below + far_below).astype(BF16), 3).astype(F32)
    return here + above + below


def solution(mesh):
    placed = (
        P(None, "sec", None, None),
        P("op", None, None),
        P("op", None, None),
        P("op", "sec", None),
    )
    return jax.shard_map(
        shards, mesh=mesh, in_specs=placed, out_specs=P(None, "sec", "op", None), check_vma=False
    )
```

```python
import jax
import jax.numpy as jnp
from jax import lax
from jax.experimental import pallas as pl
from jax.experimental.pallas import tpu as pltpu
from jax.sharding import PartitionSpec as P

F32, BF16 = jnp.float32, jnp.bfloat16
RING = 16
LEADERS = (0, 3, -3, 6, -6)
ORDER = [1 - p for p in LEADERS] + [-1 - p for p in LEADERS] + [8] + [-p for p in LEADERS]


def split_kernel(psi, *rest):
    outs, sems = rest[:-1], rest[-1]
    copies = [pltpu.make_async_copy(psi.at[v], out, sems.at[v]) for v, out in enumerate(outs)]
    for copy in copies:
        copy.start()
    for copy in copies:
        copy.wait()


def split(psi):
    vectors = psi.shape[0]
    return pl.pallas_call(
        split_kernel,
        in_specs=[pl.BlockSpec(memory_space=pl.ANY)],
        out_specs=[pl.BlockSpec(memory_space=pltpu.VMEM)] * vectors,
        out_shape=[jax.ShapeDtypeStruct(psi.shape[1:], BF16)] * vectors,
        scratch_shapes=[pltpu.SemaphoreType.DMA((vectors,))],
        compiler_params=pltpu.CompilerParams(vmem_limit_bytes=60 * 10**6),
        cost_estimate=pl.CostEstimate(flops=0, bytes_accessed=4 * 2**20, transcendentals=0),
    )(psi)


def arrange_kernel(at, left, right, left_out, right_out):
    terms, size = left.shape[0], left.shape[1]
    share = size // RING
    sign = 1 - 2 * (at[0] % 2)
    for place, j in enumerate(ORDER):
        start = pl.multiple_of(lax.rem(at[2] + sign * j + RING, RING) * share, share)
        for k in range(terms):
            left_out[pl.ds(place * share, share), pl.ds(k * size, size)] = left[
                k, pl.ds(start, share), :
            ]
    for k in range(terms):
        right_out[k] = right[k].T


def arrange(at, left, right):
    terms, size = left.shape[0], left.shape[1]
    whole = pl.BlockSpec(memory_space=pltpu.VMEM)
    return pl.pallas_call(
        arrange_kernel,
        in_specs=[pl.BlockSpec(memory_space=pltpu.SMEM), whole, whole],
        out_specs=[whole, whole],
        out_shape=[
            jax.ShapeDtypeStruct((size, terms * size), BF16),
            jax.ShapeDtypeStruct(right.shape, BF16),
        ],
        compiler_params=pltpu.CompilerParams(vmem_limit_bytes=16 * 2**20),
        cost_estimate=pl.CostEstimate(flops=0, bytes_accessed=6 * 2**20, transcendentals=0),
    )(at, left, right)


def kernel(v, place, link, across, own, chip, right, left, up, down, opposite, halved, combined):
    terms, size = right.shape[0], right.shape[1]
    first_core = place[0] % 2 == 0
    lowest, highest = place[0] == 0, place[0] == place[1] - 1
    half, tall, wide = size // 2, 16, 256

    def weight(k, j, if_first, if_second):
        reach = jnp.where(first_core, if_first, if_second)
        outside = (lowest & (reach < 2 - j)) | (highest & (reach > 3 - j))
        return jnp.where(outside, 0, link[(k * 2 + j) * 5 + reach]).astype(F32)

    reaches = (((0, 4), (2, 2), (3, 3), (4, 0), (1, 1)), ((0, 4), (1, 1), (2, 2), (4, 0), (3, 3)))
    weights = [
        [[weight(k, j, *pair) for pair in reaches[j]] for k in range(terms)] for j in range(2)
    ]

    def combine(part):
        for row in range(0, half, tall):
            rows = pl.ds(part * half + row, tall)
            for column in range(0, size, wide):
                columns = pl.ds(column, wide)
                a0, a1 = (across[i, rows, columns].astype(F32) for i in range(2))
                o0, o1 = (own[i, rows, columns].astype(F32) for i in range(2))
                c0, c1 = (chip[i, rows, columns].astype(F32) for i in range(2))
                fifth = (jnp.where(first_core, a1, c1), jnp.where(first_core, c0, a0))
                for j, blocks in enumerate(((a0, o0, o1, c0, fifth[0]), (a1, o0, o1, c1, fifth[1]))):
                    for k in range(terms):
                        total = weights[j][k][0] * blocks[0]
                        for slot in range(1, 5):
                            total += weights[j][k][slot] * blocks[slot]
                        combined[part, j * terms + k, pl.ds(row, tall), columns] = total.astype(BF16)

    def multiply_right(part):
        for j in range(2):
            for k in range(terms):
                halved[j, pl.ds(k * size + part * half, half), :] = jnp.dot(
                    combined[part, j * terms + k], right[k], preferred_element_type=F32
                ).astype(BF16)

    combine(0)
    combine(1)
    multiply_right(0)
    multiply_right(1)
    multiply_left(left, halved, (up, down, opposite), 0)


def multiply_left(left, halved, outs, first):
    last = first + sum(out.shape[1] for out in outs)
    for j in range(2):
        for top in range(first, last, 128):
            high = min(128, last - top)
            sums = jnp.dot(
                left[pl.ds(top, high), :], halved[j], preferred_element_type=F32
            ).astype(BF16)
            start = first
            for out in outs:
                end = start + out.shape[1]
                low, stop = max(top, start), min(top + high, end)
                if low < stop:
                    out[j, pl.ds(low - start, stop - low)] = sums[low - top : stop - top]
                start = end


def mine_kernel(left, halved, out):
    multiply_left(left, halved, (out,), left.shape[0] - out.shape[1])


def mine_shares(left, halved):
    size = halved.shape[2]
    rows = len(LEADERS) * (size // RING)
    whole = pl.BlockSpec(memory_space=pltpu.VMEM)
    return pl.pallas_call(
        mine_kernel,
        in_specs=[whole] * 2,
        out_specs=whole,
        out_shape=jax.ShapeDtypeStruct((2, rows, size), BF16),
        compiler_params=pltpu.CompilerParams(vmem_limit_bytes=16 * 2**20),
        cost_estimate=pl.CostEstimate(
            flops=4 * rows * halved.shape[1] * size, bytes_accessed=4 * 2**20, transcendentals=0
        ),
    )(left, halved)


def partials(v, place, link, across, own, chip, right, left):
    terms, size = right.shape[0], right.shape[1]
    share = size // RING
    whole = pl.BlockSpec(memory_space=pltpu.VMEM)
    scalars = pl.BlockSpec(memory_space=pltpu.SMEM)
    shapes = [(2, n * share, size) for n in (len(LEADERS), len(LEADERS), 1)]
    shapes.append((2, terms * size, size))
    return pl.pallas_call(
        lambda *refs: kernel(v, *refs),
        in_specs=[scalars, scalars] + [whole] * 5,
        out_specs=[whole] * 4,
        out_shape=[jax.ShapeDtypeStruct(shape, BF16) for shape in shapes],
        scratch_shapes=[
            pltpu.VMEM((2, 2 * terms, size // 2, size), BF16),
        ],
        compiler_params=pltpu.CompilerParams(vmem_limit_bytes=32 * 2**20),
        cost_estimate=pl.CostEstimate(
            flops=8 * terms * size**3, bytes_accessed=8 * 2**20, transcendentals=0
        ),
    )(place, link, across, own, chip, right, left)


def shift(x, by):
    n, m = lax.axis_size("op"), lax.axis_size("sec")
    pairs = [
        (i * m + q, (i + (-by if q % 2 else by)) % n * m + q) for i in range(n) for q in range(m)
    ]
    return lax.ppermute(x, ("op", "sec"), pairs)


def shards(psi, left_op, right_op, link):
    place = lax.axis_index("sec")
    count = lax.axis_size("sec")
    vectors = psi.shape[0]
    share = psi.shape[2] // RING
    at = jnp.stack([place, count, lax.axis_index("op")]).astype(jnp.int32)

    facing = [(i, i + 1) for i in range(1, count - 1, 2)]
    facing += [(b, a) for a, b in facing]
    own = split(psi)
    across = [lax.ppermute(block, "sec", facing) for block in own]
    chip = [lax.ppermute(block, "sec", [(i, i ^ 1) for i in range(count)]) for block in own]

    left, right = arrange(at, left_op, right_op)
    totals, opposites = [], []
    for v in range(vectors):
        up, down, opposite, halved = partials(
            v, at, link.reshape(-1), across[v], own[v], chip[v], right, left
        )
        mine = mine_shares(left, halved)
        total = mine.astype(F32) + shift(up, 1).astype(F32) + shift(down, -1).astype(F32)
        totals.append(total.reshape(2, len(LEADERS), share, -1))
        opposites.append(opposite)
    opposite = shift(jnp.stack(opposites), -2).astype(F32)
    here, above, below, far_above, far_below = (
        jnp.stack([total[:, i] for total in totals]) for i in range(len(LEADERS))
    )
    far_above = shift((far_above + opposite).astype(BF16), -3).astype(F32)
    far_below = shift(far_below.astype(BF16), 3).astype(F32)
    above = shift((above + far_above).astype(BF16), -3).astype(F32)
    below = shift((below + far_below).astype(BF16), 3).astype(F32)
    return here + above + below


def solution(mesh):
    placed = (
        P(None, "sec", None, None),
        P("op", None, None),
        P("op", None, None),
        P("op", "sec", None),
    )
    return jax.shard_map(
        shards, mesh=mesh, in_specs=placed, out_specs=P(None, "sec", "op", None), check_vma=False
    )
```

```python
import jax
import jax.numpy as jnp
from jax import lax
from jax.experimental import pallas as pl
from jax.experimental.pallas import tpu as pltpu
from jax.sharding import PartitionSpec as P

F32, BF16 = jnp.float32, jnp.bfloat16
RING = 16
LEADERS = (0, 3, -3, 6, -6)
ORDER = [1 - p for p in LEADERS] + [-1 - p for p in LEADERS] + [8] + [-p for p in LEADERS]


def split_kernel(psi, *rest):
    outs, (chunks, came, went) = rest[:-3], rest[-3:]
    parts = [(v, i, part) for v in range(len(outs)) for i in range(2) for part in range(2)]
    rows = psi.shape[2] // 2
    ways = []
    for n, (v, i, part) in enumerate(parts):
        at = pl.ds(part * rows, rows)
        ways.append(
            (
                pltpu.make_async_copy(psi.at[v, i, at], chunks.at[n], came.at[n]),
                pltpu.make_async_copy(chunks.at[n], outs[v].at[i, at], went.at[n]),
            )
        )
    for into, _ in ways:
        into.start()
    for into, out in ways:
        into.wait()
        out.start()
    for _, out in ways:
        out.wait()


def split(psi):
    vectors, _, size, _ = psi.shape
    count = 4 * vectors
    anywhere = pl.BlockSpec(memory_space=pl.ANY)
    return pl.pallas_call(
        split_kernel,
        in_specs=[anywhere],
        out_specs=[anywhere] * vectors,
        out_shape=[jax.ShapeDtypeStruct(psi.shape[1:], BF16)] * vectors,
        scratch_shapes=[
            pltpu.VMEM((count, size // 2, size), BF16),
            pltpu.SemaphoreType.DMA((count,)),
            pltpu.SemaphoreType.DMA((count,)),
        ],
        compiler_params=pltpu.CompilerParams(vmem_limit_bytes=60 * 10**6),
        cost_estimate=pl.CostEstimate(flops=0, bytes_accessed=4 * 2**20, transcendentals=0),
    )(psi)


def arrange_kernel(at, left, right, left_out, right_out):
    terms, size = left.shape[0], left.shape[1]
    share = size // RING
    sign = 1 - 2 * (at[0] % 2)
    for place, j in enumerate(ORDER):
        start = pl.multiple_of(lax.rem(at[2] + sign * j + RING, RING) * share, share)
        for k in range(terms):
            left_out[pl.ds(place * share, share), pl.ds(k * size, size)] = left[
                k, pl.ds(start, share), :
            ]
    for k in range(terms):
        right_out[k] = right[k].T


def arrange(at, left, right):
    terms, size = left.shape[0], left.shape[1]
    whole = pl.BlockSpec(memory_space=pltpu.VMEM)
    return pl.pallas_call(
        arrange_kernel,
        in_specs=[pl.BlockSpec(memory_space=pltpu.SMEM), whole, whole],
        out_specs=[whole, whole],
        out_shape=[
            jax.ShapeDtypeStruct((size, terms * size), BF16),
            jax.ShapeDtypeStruct(right.shape, BF16),
        ],
        compiler_params=pltpu.CompilerParams(vmem_limit_bytes=16 * 2**20),
        cost_estimate=pl.CostEstimate(flops=0, bytes_accessed=6 * 2**20, transcendentals=0),
    )(at, left, right)


def kernel(v, place, link, across, own, chip, right, left, up, down, opposite, halved, combined):
    terms, size = right.shape[0], right.shape[1]
    first_core = place[0] % 2 == 0
    lowest, highest = place[0] == 0, place[0] == place[1] - 1
    half, tall, wide = size // 2, 16, 256

    def weight(k, j, if_first, if_second):
        reach = jnp.where(first_core, if_first, if_second)
        outside = (lowest & (reach < 2 - j)) | (highest & (reach > 3 - j))
        return jnp.where(outside, 0, link[(k * 2 + j) * 5 + reach]).astype(F32)

    reaches = (((0, 4), (2, 2), (3, 3), (4, 0), (1, 1)), ((0, 4), (1, 1), (2, 2), (4, 0), (3, 3)))
    weights = [
        [[weight(k, j, *pair) for pair in reaches[j]] for k in range(terms)] for j in range(2)
    ]

    def combine(part):
        for row in range(0, half, tall):
            rows = pl.ds(part * half + row, tall)
            for column in range(0, size, wide):
                columns = pl.ds(column, wide)
                a0, a1 = (across[i, rows, columns].astype(F32) for i in range(2))
                o0, o1 = (own[i, rows, columns].astype(F32) for i in range(2))
                c0, c1 = (chip[i, rows, columns].astype(F32) for i in range(2))
                fifth = (jnp.where(first_core, a1, c1), jnp.where(first_core, c0, a0))
                for j, blocks in enumerate(((a0, o0, o1, c0, fifth[0]), (a1, o0, o1, c1, fifth[1]))):
                    for k in range(terms):
                        total = weights[j][k][0] * blocks[0]
                        for slot in range(1, 5):
                            total += weights[j][k][slot] * blocks[slot]
                        combined[part, j * terms + k, pl.ds(row, tall), columns] = total.astype(BF16)

    def multiply_right(part):
        for j in range(2):
            for k in range(terms):
                halved[j, pl.ds(k * size + part * half, half), :] = jnp.dot(
                    combined[part, j * terms + k], right[k], preferred_element_type=F32
                ).astype(BF16)

    combine(0)
    combine(1)
    multiply_right(0)
    multiply_right(1)
    multiply_left(left, halved, (up, down, opposite), 0)


def multiply_left(left, halved, outs, first):
    last = first + sum(out.shape[1] for out in outs)
    for j in range(2):
        for top in range(first, last, 128):
            high = min(128, last - top)
            sums = jnp.dot(
                left[pl.ds(top, high), :], halved[j], preferred_element_type=F32
            ).astype(BF16)
            start = first
            for out in outs:
                end = start + out.shape[1]
                low, stop = max(top, start), min(top + high, end)
                if low < stop:
                    out[j, pl.ds(low - start, stop - low)] = sums[low - top : stop - top]
                start = end


def mine_kernel(left, halved, out):
    multiply_left(left, halved, (out,), left.shape[0] - out.shape[1])


def mine_shares(left, halved):
    size = halved.shape[2]
    rows = len(LEADERS) * (size // RING)
    whole = pl.BlockSpec(memory_space=pltpu.VMEM)
    return pl.pallas_call(
        mine_kernel,
        in_specs=[whole] * 2,
        out_specs=whole,
        out_shape=jax.ShapeDtypeStruct((2, rows, size), BF16),
        compiler_params=pltpu.CompilerParams(vmem_limit_bytes=16 * 2**20),
        cost_estimate=pl.CostEstimate(
            flops=4 * rows * halved.shape[1] * size, bytes_accessed=4 * 2**20, transcendentals=0
        ),
    )(left, halved)


def partials(v, place, link, across, own, chip, right, left):
    terms, size = right.shape[0], right.shape[1]
    share = size // RING
    whole = pl.BlockSpec(memory_space=pltpu.VMEM)
    scalars = pl.BlockSpec(memory_space=pltpu.SMEM)
    shapes = [(2, n * share, size) for n in (len(LEADERS), len(LEADERS), 1)]
    shapes.append((2, terms * size, size))
    return pl.pallas_call(
        lambda *refs: kernel(v, *refs),
        in_specs=[scalars, scalars] + [whole] * 5,
        out_specs=[whole] * 4,
        out_shape=[jax.ShapeDtypeStruct(shape, BF16) for shape in shapes],
        scratch_shapes=[
            pltpu.VMEM((2, 2 * terms, size // 2, size), BF16),
        ],
        compiler_params=pltpu.CompilerParams(vmem_limit_bytes=32 * 2**20),
        cost_estimate=pl.CostEstimate(
            flops=8 * terms * size**3, bytes_accessed=8 * 2**20, transcendentals=0
        ),
    )(place, link, across, own, chip, right, left)


def shift(x, by):
    n, m = lax.axis_size("op"), lax.axis_size("sec")
    pairs = [
        (i * m + q, (i + (-by if q % 2 else by)) % n * m + q) for i in range(n) for q in range(m)
    ]
    return lax.ppermute(x, ("op", "sec"), pairs)


def shards(psi, left_op, right_op, link):
    place = lax.axis_index("sec")
    count = lax.axis_size("sec")
    vectors = psi.shape[0]
    share = psi.shape[2] // RING
    at = jnp.stack([place, count, lax.axis_index("op")]).astype(jnp.int32)

    facing = [(i, i + 1) for i in range(1, count - 1, 2)]
    facing += [(b, a) for a, b in facing]
    own = split(psi)
    across = [lax.ppermute(block, "sec", facing) for block in own]
    chip = [lax.ppermute(block, "sec", [(i, i ^ 1) for i in range(count)]) for block in own]

    left, right = arrange(at, left_op, right_op)
    totals, opposites = [], []
    for v in range(vectors):
        up, down, opposite, halved = partials(
            v, at, link.reshape(-1), across[v], own[v], chip[v], right, left
        )
        mine = mine_shares(left, halved)
        total = mine.astype(F32) + shift(up, 1).astype(F32) + shift(down, -1).astype(F32)
        totals.append(total.reshape(2, len(LEADERS), share, -1))
        opposites.append(opposite)
    opposite = shift(jnp.stack(opposites), -2).astype(F32)
    here, above, below, far_above, far_below = (
        jnp.stack([total[:, i] for total in totals]) for i in range(len(LEADERS))
    )
    far_above = shift((far_above + opposite).astype(BF16), -3).astype(F32)
    far_below = shift(far_below.astype(BF16), 3).astype(F32)
    above = shift((above + far_above).astype(BF16), -3).astype(F32)
    below = shift((below + far_below).astype(BF16), 3).astype(F32)
    return here + above + below


def solution(mesh):
    placed = (
        P(None, "sec", None, None),
        P("op", None, None),
        P("op", None, None),
        P("op", "sec", None),
    )
    return jax.shard_map(
        shards, mesh=mesh, in_specs=placed, out_specs=P(None, "sec", "op", None), check_vma=False
    )
```

```python
import jax
import jax.numpy as jnp
from jax import lax
from jax.experimental import pallas as pl
from jax.experimental.pallas import tpu as pltpu
from jax.sharding import PartitionSpec as P

F32, BF16 = jnp.float32, jnp.bfloat16
RING = 16
LEADERS = (0, 3, -3, 6, -6)
ORDER = [1 - p for p in LEADERS] + [-1 - p for p in LEADERS] + [8] + [-p for p in LEADERS]


def take(psi, v):
    size = psi.shape[2]
    count = 4
    rows = 2 * size // count

    def kernel(source, out, chunks, came, went):
        ways = []
        for n in range(count):
            at = (n * rows // size, pl.ds(n * rows % size, rows))
            ways.append(
                (
                    pltpu.make_async_copy(source.at[(v,) + at], chunks.at[n], came.at[n]),
                    pltpu.make_async_copy(chunks.at[n], out.at[at], went.at[n]),
                )
            )
        for into, _ in ways:
            into.start()
        for into, way in ways:
            into.wait()
            way.start()
        for _, way in ways:
            way.wait()

    anywhere = pl.BlockSpec(memory_space=pl.ANY)
    return pl.pallas_call(
        kernel,
        in_specs=[anywhere],
        out_specs=anywhere,
        out_shape=jax.ShapeDtypeStruct(psi.shape[1:], BF16),
        scratch_shapes=[
            pltpu.VMEM((count, rows, size), BF16),
            pltpu.SemaphoreType.DMA((count,)),
            pltpu.SemaphoreType.DMA((count,)),
        ],
        compiler_params=pltpu.CompilerParams(vmem_limit_bytes=60 * 10**6),
        cost_estimate=pl.CostEstimate(flops=0, bytes_accessed=2 * 2**20, transcendentals=0),
    )(psi)


def arrange_kernel(at, left, right, left_out, right_out):
    terms, size = left.shape[0], left.shape[1]
    share = size // RING
    sign = 1 - 2 * (at[0] % 2)
    for place, j in enumerate(ORDER):
        start = pl.multiple_of(lax.rem(at[2] + sign * j + RING, RING) * share, share)
        for k in range(terms):
            left_out[pl.ds(place * share, share), pl.ds(k * size, size)] = left[
                k, pl.ds(start, share), :
            ]
    for k in range(terms):
        right_out[k] = right[k].T


def arrange(at, left, right):
    terms, size = left.shape[0], left.shape[1]
    whole = pl.BlockSpec(memory_space=pltpu.VMEM)
    return pl.pallas_call(
        arrange_kernel,
        in_specs=[pl.BlockSpec(memory_space=pltpu.SMEM), whole, whole],
        out_specs=[whole, whole],
        out_shape=[
            jax.ShapeDtypeStruct((size, terms * size), BF16),
            jax.ShapeDtypeStruct(right.shape, BF16),
        ],
        compiler_params=pltpu.CompilerParams(vmem_limit_bytes=16 * 2**20),
        cost_estimate=pl.CostEstimate(flops=0, bytes_accessed=6 * 2**20, transcendentals=0),
    )(at, left, right)


def kernel(v, place, link, across, own, chip, right, left, up, down, opposite, halved, combined):
    terms, size = right.shape[0], right.shape[1]
    first_core = place[0] % 2 == 0
    lowest, highest = place[0] == 0, place[0] == place[1] - 1
    half, tall, wide = size // 2, 16, 256

    def weight(k, j, if_first, if_second):
        reach = jnp.where(first_core, if_first, if_second)
        outside = (lowest & (reach < 2 - j)) | (highest & (reach > 3 - j))
        return jnp.where(outside, 0, link[(k * 2 + j) * 5 + reach]).astype(F32)

    reaches = (((0, 4), (2, 2), (3, 3), (4, 0), (1, 1)), ((0, 4), (1, 1), (2, 2), (4, 0), (3, 3)))
    weights = [
        [[weight(k, j, *pair) for pair in reaches[j]] for k in range(terms)] for j in range(2)
    ]

    def combine(part):
        for row in range(0, half, tall):
            rows = pl.ds(part * half + row, tall)
            for column in range(0, size, wide):
                columns = pl.ds(column, wide)
                a0, a1 = (across[i, rows, columns].astype(F32) for i in range(2))
                o0, o1 = (own[i, rows, columns].astype(F32) for i in range(2))
                c0, c1 = (chip[i, rows, columns].astype(F32) for i in range(2))
                fifth = (jnp.where(first_core, a1, c1), jnp.where(first_core, c0, a0))
                for j, blocks in enumerate(((a0, o0, o1, c0, fifth[0]), (a1, o0, o1, c1, fifth[1]))):
                    for k in range(terms):
                        total = weights[j][k][0] * blocks[0]
                        for slot in range(1, 5):
                            total += weights[j][k][slot] * blocks[slot]
                        combined[part, j * terms + k, pl.ds(row, tall), columns] = total.astype(BF16)

    def multiply_right(part):
        for j in range(2):
            for k in range(terms):
                halved[j, pl.ds(k * size + part * half, half), :] = jnp.dot(
                    combined[part, j * terms + k], right[k], preferred_element_type=F32
                ).astype(BF16)

    combine(0)
    combine(1)
    multiply_right(0)
    multiply_right(1)
    multiply_left(left, halved, (up, down, opposite), 0)


def multiply_left(left, halved, outs, first):
    last = first + sum(out.shape[1] for out in outs)
    for j in range(2):
        for top in range(first, last, 128):
            high = min(128, last - top)
            sums = jnp.dot(
                left[pl.ds(top, high), :], halved[j], preferred_element_type=F32
            ).astype(BF16)
            start = first
            for out in outs:
                end = start + out.shape[1]
                low, stop = max(top, start), min(top + high, end)
                if low < stop:
                    out[j, pl.ds(low - start, stop - low)] = sums[low - top : stop - top]
                start = end


def mine_kernel(left, halved, out):
    multiply_left(left, halved, (out,), left.shape[0] - out.shape[1])


def mine_shares(left, halved):
    size = halved.shape[2]
    rows = len(LEADERS) * (size // RING)
    whole = pl.BlockSpec(memory_space=pltpu.VMEM)
    return pl.pallas_call(
        mine_kernel,
        in_specs=[whole] * 2,
        out_specs=whole,
        out_shape=jax.ShapeDtypeStruct((2, rows, size), BF16),
        compiler_params=pltpu.CompilerParams(vmem_limit_bytes=16 * 2**20),
        cost_estimate=pl.CostEstimate(
            flops=4 * rows * halved.shape[1] * size, bytes_accessed=4 * 2**20, transcendentals=0
        ),
    )(left, halved)


def partials(v, place, link, across, own, chip, right, left):
    terms, size = right.shape[0], right.shape[1]
    share = size // RING
    whole = pl.BlockSpec(memory_space=pltpu.VMEM)
    scalars = pl.BlockSpec(memory_space=pltpu.SMEM)
    shapes = [(2, n * share, size) for n in (len(LEADERS), len(LEADERS), 1)]
    shapes.append((2, terms * size, size))
    return pl.pallas_call(
        lambda *refs: kernel(v, *refs),
        in_specs=[scalars, scalars] + [whole] * 5,
        out_specs=[whole] * 4,
        out_shape=[jax.ShapeDtypeStruct(shape, BF16) for shape in shapes],
        scratch_shapes=[
            pltpu.VMEM((2, 2 * terms, size // 2, size), BF16),
        ],
        compiler_params=pltpu.CompilerParams(vmem_limit_bytes=32 * 2**20),
        cost_estimate=pl.CostEstimate(
            flops=8 * terms * size**3, bytes_accessed=8 * 2**20, transcendentals=0
        ),
    )(place, link, across, own, chip, right, left)


def shift(x, by):
    n, m = lax.axis_size("op"), lax.axis_size("sec")
    pairs = [
        (i * m + q, (i + (-by if q % 2 else by)) % n * m + q) for i in range(n) for q in range(m)
    ]
    return lax.ppermute(x, ("op", "sec"), pairs)


def shards(psi, left_op, right_op, link):
    place = lax.axis_index("sec")
    count = lax.axis_size("sec")
    vectors = psi.shape[0]
    share = psi.shape[2] // RING
    at = jnp.stack([place, count, lax.axis_index("op")]).astype(jnp.int32)

    facing = [(i, i + 1) for i in range(1, count - 1, 2)]
    facing += [(b, a) for a, b in facing]
    own = [take(psi, v) for v in range(vectors)]
    across = [lax.ppermute(block, "sec", facing) for block in own]
    chip = [lax.ppermute(block, "sec", [(i, i ^ 1) for i in range(count)]) for block in own]

    left, right = arrange(at, left_op, right_op)
    totals, opposites = [], []
    for v in range(vectors):
        up, down, opposite, halved = partials(
            v, at, link.reshape(-1), across[v], own[v], chip[v], right, left
        )
        mine = mine_shares(left, halved)
        total = mine.astype(F32) + shift(up, 1).astype(F32) + shift(down, -1).astype(F32)
        totals.append(total.reshape(2, len(LEADERS), share, -1))
        opposites.append(opposite)
    opposite = shift(jnp.stack(opposites), -2).astype(F32)
    here, above, below, far_above, far_below = (
        jnp.stack([total[:, i] for total in totals]) for i in range(len(LEADERS))
    )
    far_above = shift((far_above + opposite).astype(BF16), -3).astype(F32)
    far_below = shift(far_below.astype(BF16), 3).astype(F32)
    above = shift((above + far_above).astype(BF16), -3).astype(F32)
    below = shift((below + far_below).astype(BF16), 3).astype(F32)
    return here + above + below


def solution(mesh):
    placed = (
        P(None, "sec", None, None),
        P("op", None, None),
        P("op", None, None),
        P("op", "sec", None),
    )
    return jax.shard_map(
        shards, mesh=mesh, in_specs=placed, out_specs=P(None, "sec", "op", None), check_vma=False
    )
```
